512 devices in a mesh: grp: 8 (over y, core), blk: 64 (over x, z).
Axes of the slice: x: 4, y: 4, z: 16, core: 2. Of those that a mesh axis runs over, the one named last changes fastest.
Arguments:
- panels: float32 [64, 16, 8192], P('blk', 'grp'), may hold values from -6 to 6
- routes: int32 [64, 16, 32], P('blk', 'grp'), may hold values from 0 to 63, all different within a row
- stack_in: float32 [8, 64, 128, 16, 128], P('grp', 'blk'), may hold values from -6 to 6
Outputs:
- stack_out: float32 [8, 64, 128, 16, 128], P('grp', 'blk')
The draws below stay inside these ranges and needn't reach their ends.
Inputs may be any that keep to these rules, and one draw needn't show every extreme that they name: `routes`: each channel names 32 different receiver groups; every group is named by some channel.
All inputs are finite; a program needn't handle non-finite values.
Results may differ from the reference program's by a relative error of at most 0.003.
Values may be sent and summed in bfloat16 or wider, within the bound.
No kernel may reach another device: no remote copies, remote signals or barrier semaphores. Data moves between devices by JAX's collectives and lax.ppermute only.
A program may use at most 64 MiB of HBM per device.

```python
import math
import jax
import jax.numpy as jnp
from jax import lax

NF = 4096
LAGS = 128
SMOOTH = 64
CH_DEV = 2
GROUPW = 16
SOURCES = 128
TOPS = 32
N_GRP = 8
N_BLK = 64


def block_levels(key, extent, split, low, high):
    factor_of, own = 1.0, jax.random.fold_in(key, 6)
    for position, parts in split:
        draws = jnp.exp(jax.random.uniform(jax.random.fold_in(own, position), (parts,), jnp.float32, low / len(split), high / len(split)))
        factor_of = factor_of * jnp.repeat(draws, extent[position] // parts).reshape([-1 if axis == position else 1 for axis in range(len(extent))])
    return factor_of


def different_ones(rng, rows, amount, top, lift):
    sequence = jax.random.permutation(jax.random.fold_in(rng, 1), amount)
    pull = sequence
    for power in range(3):
        pull = pull * pull // amount
    pull = pull * lift // amount
    lots = jax.random.randint(jax.random.fold_in(rng, 2), (rows, amount), 0, 4096) + pull
    sure = jax.random.permutation(jax.random.fold_in(rng, 3), rows)[jnp.arange(amount) % rows]
    lots = jnp.where(jnp.arange(rows)[:, None] == sure[None, :], 1 << 14, lots)
    priority = lots * amount + jnp.arange(amount)
    return lax.top_k(priority.astype(jnp.int32), top)[1].astype(jnp.int32)


def scatter_about(key, dims, scale, limit, pieces=(), held_as=jnp.bfloat16):
    gain = block_levels(key, dims, pieces, -0.22, 0.18) if pieces else 1.0
    array = jax.random.normal(key, dims, jnp.float32) * scale * gain
    return jnp.minimum(jnp.maximum(array, -limit), limit).astype(held_as)


def setup_inputs(seed: int = 0) -> dict:
    keys = jax.random.split(jax.random.key(seed), 4)
    panels = scatter_about(keys[0], (N_BLK, GROUPW, 2 * NF), 1.0, 6.0, ((0, 64), (1, 8)), jnp.float32)
    routes = different_ones(keys[1], N_BLK * GROUPW, N_BLK, TOPS, 8192).reshape((N_BLK, GROUPW, TOPS))
    stack_in = scatter_about(keys[2], (N_GRP, N_BLK, SOURCES, GROUPW, LAGS), 1.0, 6.0, ((0, 8), (1, 64)), jnp.float32)
    return {"panels": panels, "routes": routes, "stack_in": stack_in}


def whiten(spectra):
    real_part = spectra[:, :NF]
    imag_part = spectra[:, NF:]
    amplitude = jnp.sqrt(real_part * real_part + imag_part * imag_part)
    padded = jnp.pad(amplitude, ((0, 0), (SMOOTH + 1, SMOOTH)))
    running = jnp.cumsum(padded, axis=1)
    smoothed = (running[:, 2 * SMOOTH + 1:] - running[:, :NF]) / (2 * SMOOTH + 1)
    divisor = smoothed + 1e-06
    return jnp.concatenate([real_part / divisor, imag_part / divisor], axis=1).astype(jnp.bfloat16)

def make_table():
    frequency = jnp.arange(NF, dtype=jnp.int32)
    lag_values = jnp.arange(LAGS, dtype=jnp.int32) - LAGS // 2
    phase_index = frequency[:, None] * lag_values[None, :] % (2 * NF)
    angles = phase_index.astype(jnp.float32) * (math.pi / NF)
    return jnp.concatenate([jnp.cos(angles), -jnp.sin(angles)], axis=0).astype(jnp.bfloat16)

def correlate(sources, receivers, dft_table):
    source_re = sources[:, :NF].astype(jnp.float32)
    source_im = sources[:, NF:].astype(jnp.float32)
    recv_re = receivers[:, :NF].astype(jnp.float32)
    recv_im = receivers[:, NF:].astype(jnp.float32)
    cross_re = source_re[:, None, :] * recv_re[None] + source_im[:, None, :] * recv_im[None]
    cross_im = source_im[:, None, :] * recv_re[None] - source_re[:, None, :] * recv_im[None]
    cross_spectra = jnp.concatenate([cross_re, cross_im], axis=2).astype(jnp.bfloat16)
    count_src = sources.shape[0]
    count_recv = receivers.shape[0]
    flat = cross_spectra.reshape(count_src * count_recv, 2 * NF)
    correlogram = jnp.dot(flat, dft_table, preferred_element_type=jnp.float32) * (1.0 / math.sqrt(NF))
    return correlogram.reshape(count_src, count_recv, LAGS)

def reference(panels, routes, stack_in):
    whitened = whiten(panels.reshape(N_BLK * GROUPW, 2 * NF)).reshape(N_BLK, GROUPW, 2 * NF)
    dft_table = make_table()
    results = []
    for group_index in range(N_GRP):
        sources = whitened[:, group_index * CH_DEV:(group_index + 1) * CH_DEV].reshape(SOURCES, 2 * NF)
        source_routes = routes[:, group_index * CH_DEV:(group_index + 1) * CH_DEV].reshape(SOURCES, TOPS)

        def owner_work(pair):
            owner_index, previous = pair
            receivers = whitened[owner_index]
            live_mask = jnp.any(source_routes == owner_index, axis=1).astype(jnp.float32)
            correlogram = correlate(sources, receivers, dft_table)
            return previous + live_mask[:, None, None] * correlogram
        results.append(lax.map(owner_work, (jnp.arange(N_BLK, dtype=jnp.int32), stack_in[group_index])))
    return jnp.stack(results, axis=0)
```

```python
import functools
import math

import jax
import jax.numpy as jnp
import numpy as np
from jax import lax
from jax.experimental import pallas as pl
from jax.experimental.pallas import tpu as pltpu
from jax.sharding import Mesh, PartitionSpec as P

NF = 4096
LAGS = 128
HALF = LAGS // 2
SMOOTH = 64
LANES = 128
SLICES = 2 * NF // LANES
CH = 2
ROUTE_LANES = 128


def tables():
    frequency = np.arange(NF, dtype=np.int64)

    def angle(t):
        return (frequency[None, :] * np.asarray(t)[:, None] % (2 * NF)) * (math.pi / NF)

    cos = np.cos(angle(np.arange(HALF)))
    sin = np.sin(angle(HALF - np.arange(HALF)))
    edge = np.zeros((16, NF))
    edge[0] = np.cos(angle([HALF]))[0]
    return tuple(a.astype(np.float32).astype(jnp.bfloat16) for a in (cos, sin, edge))


def whiten_kernel(panels_ref, routes_ref, out_ref):
    real = panels_ref[:, :NF]
    imag = panels_ref[:, NF:]
    amplitude = jnp.sqrt(real * real + imag * imag)
    wide = NF + 2 * SMOOTH
    padded = jnp.concatenate([amplitude, jnp.zeros((CH, 2 * SMOOTH), jnp.float32)], axis=1)
    total = padded
    span = 1
    while span < 2 * SMOOTH:
        total = total + pltpu.roll(total, span, 1)
        span *= 2
    total = total + pltpu.roll(padded, 2 * SMOOTH, 1)
    total = pltpu.roll(total, wide - SMOOTH, 1)[:, :NF]
    divisor = total / (2 * SMOOTH + 1) + 1e-06
    real = real / divisor
    imag = imag / divisor
    half = SLICES // 2
    for j in range(half):
        lanes = slice(j * LANES, (j + 1) * LANES)
        out_ref[j] = real[:, lanes].astype(jnp.bfloat16)
        out_ref[half + j] = imag[:, lanes].astype(jnp.bfloat16)
    routes = routes_ref[...].astype(jnp.float32)
    rest = jnp.full((CH, ROUTE_LANES - routes.shape[1]), -1.0, jnp.float32)
    out_ref[SLICES] = jnp.concatenate([routes, rest], axis=1).astype(jnp.bfloat16)


def whiten(panels, routes):
    return pl.pallas_call(
        whiten_kernel,
        out_shape=jax.ShapeDtypeStruct((SLICES + 1, CH, LANES), jnp.bfloat16),
        cost_estimate=pl.CostEstimate(flops=1 << 20, bytes_accessed=100000, transcendentals=0),
    )(panels, routes)


def steer_kernel(recv_ref, cos_ref, sin_ref, edge_ref, out_ref):
    receivers = out_ref.shape[0]
    half = SLICES // 2

    def step(j, carry):
        lanes = pl.ds(pl.multiple_of(j * LANES, LANES), LANES)
        upper = pl.ds(pl.multiple_of(NF + j * LANES, LANES), LANES)
        cos = cos_ref[:, lanes]
        sin = sin_ref[:, lanes]
        edge = edge_ref[:, lanes]
        for r in range(receivers):
            re32 = jnp.broadcast_to(recv_ref[pl.ds(r * SLICES + j, 1), :], (16, LANES))
            im32 = jnp.broadcast_to(recv_ref[pl.ds(r * SLICES + half + j, 1), :], (16, LANES))
            re = re32.astype(jnp.bfloat16)
            im = im32.astype(jnp.bfloat16)
            neg = -im
            for q in range(HALF // 16):
                rows = slice(16 * q, 16 * q + 16)
                low_a = neg * sin[rows]
                low_b = re * sin[rows]
                if q == 0:
                    low_a = low_a + re * edge
                    low_b = low_b + im * edge
                out_ref[r, rows, lanes] = low_a
                out_ref[r, rows, upper] = low_b
                high = slice(HALF + 16 * q, HALF + 16 * q + 16)
                out_ref[r, high, lanes] = re * cos[rows]
                out_ref[r, high, upper] = im * cos[rows]
        return carry

    lax.fori_loop(0, half, step, 0)


def steer(receivers, cos, sin, edge):
    count = receivers.shape[0] // SLICES
    return pl.pallas_call(
        steer_kernel,
        out_shape=pltpu.VMEM((count, LAGS, 2 * NF), jnp.bfloat16),
        in_specs=[pl.BlockSpec(memory_space=pltpu.VMEM)] * 4,
        out_specs=pl.BlockSpec(memory_space=pltpu.VMEM),
        compiler_params=pltpu.CompilerParams(vmem_limit_bytes=8 << 20),
        cost_estimate=pl.CostEstimate(flops=1 << 24, bytes_accessed=1 << 24, transcendentals=0),
    )(receivers, cos, sin, edge)


def stack_kernel(hops, own_ref, first_ref, second_ref, third_ref, steer_ref, stack_ref, out_ref, held_ref):
    parts = (own_ref, first_ref, second_ref, third_ref)
    _, rows, _ = own_ref.shape
    count = len(parts) * rows
    x = lax.axis_index("x")
    n_x = lax.axis_size("x")
    owner = x * lax.axis_size("z") + lax.axis_index("z")
    scales = []
    for i, part in enumerate(parts):
        for j in range(SLICES):
            held_ref[i * rows : (i + 1) * rows, j * LANES : (j + 1) * LANES] = part[j]
        routes = part[SLICES].astype(jnp.float32)
        named = jnp.where(routes == owner.astype(jnp.float32), 1.0, 0.0)
        scales.append(jnp.max(named, axis=1, keepdims=True) * (1.0 / math.sqrt(NF)))
    column = lax.broadcasted_iota(jnp.int32, (rows, LAGS), 1)
    mirror = (LAGS - column) % LAGS
    sign = jnp.where(column > HALF, -1.0, 1.0)
    sign = jnp.where((column == 0) | (column == HALF), 0.0, sign)

    for p in range(steer_ref.shape[0] // 2):
        weights = steer_ref[2 * p : 2 * p + 2].reshape(2 * LAGS, 2 * NF)
        sums = lax.dot_general(
            held_ref[...], weights, (((1,), (1,)), ((), ())), preferred_element_type=jnp.float32
        )
        for i, hop in enumerate(hops):
            base = lax.rem(x + n_x - hop, n_x) * rows
            for k in range(2):
                r = 2 * p + k
                part = sums[i * rows : (i + 1) * rows, k * LAGS : (k + 1) * LAGS]
                turned = jnp.take_along_axis(part, mirror, axis=1)
                place = (pl.ds(base, rows), r, slice(None))
                out_ref[place] = stack_ref[place] + scales[i] * (part + sign * turned)


def stack(hops, sources, steering, previous):
    count = len(sources) * sources[0].shape[1]
    return pl.pallas_call(
        functools.partial(stack_kernel, hops),
        out_shape=jax.ShapeDtypeStruct(previous.shape, jnp.float32),
        in_specs=[pl.BlockSpec(memory_space=pltpu.VMEM)] * 6,
        out_specs=pl.BlockSpec(memory_space=pltpu.VMEM),
        scratch_shapes=[pltpu.VMEM((count, 2 * NF), jnp.bfloat16)],
        compiler_params=pltpu.CompilerParams(vmem_limit_bytes=16 << 20),
        cost_estimate=pl.CostEstimate(flops=1 << 32, bytes_accessed=1 << 22, transcendentals=0),
    )(*sources, steering, previous)


def local(panels, routes, stack_in):
    n_z = lax.axis_size("z")
    n_x = lax.axis_size("x")
    payload = whiten(panels[0], routes[0])
    column = lax.all_gather(payload, "z", axis=0, tiled=False)
    column = column.transpose(1, 0, 2, 3).reshape(SLICES + 1, n_z * CH, LANES)
    hops = (0, 1, 3, 2)
    sources = [column]
    for hop in hops[1:]:
        pairs = [(i, (i + hop) % n_x) for i in range(n_x)]
        sources.append(lax.ppermute(column, "x", pairs))
    group = lax.all_gather(payload[:SLICES], ("y", "core"), axis=0, tiled=False)
    receivers = group.transpose(0, 2, 1, 3).reshape(-1, LANES).astype(jnp.float32)
    cos, sin, edge = tables()
    steering = steer(receivers, cos, sin, edge)
    return stack(hops, sources, steering, stack_in[0, 0])[None, None]


def solution(mesh):
    grid = Mesh(mesh.devices.reshape(-1, 2, 4, 16), ("y", "core", "x", "z"))
    grp, blk = ("y", "core"), ("x", "z")
    return jax.shard_map(
        local,
        mesh=grid,
        in_specs=(P(blk, grp, None), P(blk, grp, None), P(grp, blk, None, None, None)),
        out_specs=P(grp, blk, None, None, None),
        check_vma=False,
    )
```

```python
import functools
import math

import jax
import jax.numpy as jnp
import numpy as np
from jax import lax
from jax.experimental import pallas as pl
from jax.experimental.pallas import tpu as pltpu
from jax.sharding import Mesh, PartitionSpec as P

NF = 4096
LAGS = 128
HALF = LAGS // 2
SMOOTH = 64
LANES = 128
SLICES = 2 * NF // LANES
CH = 2
ROUTE_LANES = 128


def tables():
    frequency = np.arange(NF, dtype=np.int64)[:, None]
    lag = np.abs(np.arange(LAGS) - HALF)[None, :]
    angle = (frequency * lag % (2 * NF)) * (math.pi / NF)
    column = np.arange(LAGS)[None, :]
    cos = np.where((column >= HALF) | (column == 0), np.cos(angle), 0.0)
    sin = np.where(column < HALF, np.sin(angle), 0.0)
    return np.stack([cos, sin]).astype(np.float32).astype(jnp.bfloat16)


def whiten_kernel(panels_ref, routes_ref, out_ref):
    real = panels_ref[:, :NF]
    imag = panels_ref[:, NF:]
    amplitude = jnp.sqrt(real * real + imag * imag)
    wide = NF + 2 * SMOOTH
    padded = jnp.concatenate([amplitude, jnp.zeros((CH, 2 * SMOOTH), jnp.float32)], axis=1)
    total = padded
    span = 1
    while span < 2 * SMOOTH:
        total = total + pltpu.roll(total, span, 1)
        span *= 2
    total = total + pltpu.roll(padded, 2 * SMOOTH, 1)
    total = pltpu.roll(total, wide - SMOOTH, 1)[:, :NF]
    divisor = total / (2 * SMOOTH + 1) + 1e-06
    real = real / divisor
    imag = imag / divisor
    half = SLICES // 2
    for j in range(half):
        lanes = slice(j * LANES, (j + 1) * LANES)
        out_ref[j] = real[:, lanes].astype(jnp.bfloat16)
        out_ref[half + j] = imag[:, lanes].astype(jnp.bfloat16)
    routes = routes_ref[...].astype(jnp.float32)
    rest = jnp.full((CH, ROUTE_LANES - routes.shape[1]), -1.0, jnp.float32)
    out_ref[SLICES] = jnp.concatenate([routes, rest], axis=1).astype(jnp.bfloat16)


def whiten(panels, routes):
    return pl.pallas_call(
        whiten_kernel,
        out_shape=jax.ShapeDtypeStruct((SLICES + 1, CH, LANES), jnp.bfloat16),
        cost_estimate=pl.CostEstimate(flops=1 << 20, bytes_accessed=100000, transcendentals=0),
    )(panels, routes)


def steer_kernel(recv_ref, table_ref, out_ref, held_ref, sems):
    half = SLICES // 2
    receivers = recv_ref.shape[0] // SLICES
    chunks = sems.shape[0]
    rows = NF // chunks

    def fetch(c):
        part = pl.ds(c * rows, rows)
        return pltpu.make_async_copy(table_ref.at[:, part], held_ref.at[:, part], sems.at[c])

    for c in range(chunks):
        fetch(c).start()

    def step(j, carry):
        lower = pl.ds(pl.multiple_of(j * LANES, LANES), LANES)
        upper = pl.ds(pl.multiple_of(NF + j * LANES, LANES), LANES)
        re = recv_ref[pl.ds(j, receivers, stride=SLICES), :]
        im = recv_ref[pl.ds(half + j, receivers, stride=SLICES), :]
        turned = jnp.concatenate([re, im], axis=0).T.astype(jnp.bfloat16)
        cos = held_ref[0, lower, :]
        sin = held_ref[1, lower, :]
        for r in range(receivers):
            real = jnp.broadcast_to(turned[:, r : r + 1], (LANES, LAGS))
            imag = jnp.broadcast_to(turned[:, receivers + r : receivers + r + 1], (LANES, LAGS))
            lanes = slice(r % 2 * LAGS, r % 2 * LAGS + LAGS)
            out_ref[r // 2, lower, lanes] = real * cos - imag * sin
            out_ref[r // 2, upper, lanes] = imag * cos + real * sin
        return carry

    for c in range(chunks):
        fetch(c).wait()
        lax.fori_loop(c * half // chunks, (c + 1) * half // chunks, step, 0)


def steer(receivers, table):
    count = receivers.shape[0] // SLICES
    return pl.pallas_call(
        steer_kernel,
        out_shape=pltpu.VMEM((count // 2, 2 * NF, 2 * LAGS), jnp.bfloat16),
        in_specs=[pl.BlockSpec(memory_space=pltpu.VMEM), pl.BlockSpec(memory_space=pltpu.HBM)],
        out_specs=pl.BlockSpec(memory_space=pltpu.VMEM),
        scratch_shapes=[pltpu.VMEM((2, NF, LAGS), jnp.bfloat16), pltpu.SemaphoreType.DMA((4,))],
        compiler_params=pltpu.CompilerParams(vmem_limit_bytes=8 << 20),
        cost_estimate=pl.CostEstimate(flops=1 << 24, bytes_accessed=1 << 24, transcendentals=0),
    )(receivers, table)


def stack_kernel(hops, *refs):
    count = len(hops)
    parts = refs[:count]
    steer_ref, stack_ref = refs[count : count + 2]
    out_ref, held_ref, before_ref, after_ref, in_sem, out_sem = refs[-6:]
    rows = parts[0].shape[1]
    x = lax.axis_index("x")
    n_x = lax.axis_size("x")
    owner = x * lax.axis_size("z") + lax.axis_index("z")
    places = [pl.ds(lax.rem(x + n_x - hop, n_x) * rows, rows) for hop in hops]

    def fetch(i):
        return pltpu.make_async_copy(stack_ref.at[places[i]], before_ref.at[i], in_sem.at[i])

    def write(i):
        return pltpu.make_async_copy(after_ref.at[i], out_ref.at[places[i]], out_sem.at[i])

    scales = []
    for i, part in enumerate(parts):
        fetch(i).start()
        for j in range(SLICES):
            held_ref[i * rows : (i + 1) * rows, j * LANES : (j + 1) * LANES] = part[j]
        routes = part[SLICES].astype(jnp.float32)
        named = jnp.where(routes == owner.astype(jnp.float32), 1.0, 0.0)
        scales.append(jnp.max(named, axis=1, keepdims=True) * (1.0 / math.sqrt(NF)))
    column = lax.broadcasted_iota(jnp.int32, (rows, LAGS), 1)
    mirror = (LAGS - column) % LAGS
    sign = jnp.where(column > HALF, -1.0, 1.0)
    sign = jnp.where((column == 0) | (column == HALF), 0.0, sign)
    for i in range(count):
        fetch(i).wait()

    for p in range(steer_ref.shape[0]):
        sums = jnp.dot(held_ref[...], steer_ref[p], preferred_element_type=jnp.float32)
        for i in range(count):
            for k in range(2):
                part = sums[i * rows : (i + 1) * rows, k * LAGS : (k + 1) * LAGS]
                turned = jnp.take_along_axis(part, mirror, axis=1)
                after_ref[i, :, 2 * p + k, :] = before_ref[i, :, 2 * p + k, :] + scales[i] * (part + sign * turned)
    for i in range(count):
        write(i).start()
    for i in range(count):
        write(i).wait()


def stack(hops, sources, steering, previous, partial=None):
    count = len(hops)
    rows = sources[0].shape[1]
    vmem, other = pl.BlockSpec(memory_space=pltpu.VMEM), pl.BlockSpec(memory_space=pl.ANY)
    args = [*sources, steering, previous] + ([] if partial is None else [partial])
    block = (count, rows) + previous.shape[1:]
    return pl.pallas_call(
        functools.partial(stack_kernel, hops),
        out_shape=jax.ShapeDtypeStruct(previous.shape, jnp.float32),
        in_specs=[vmem] * (count + 1) + [other] * (len(args) - count - 1),
        out_specs=other,
        input_output_aliases={} if partial is None else {len(args) - 1: 0},
        scratch_shapes=[
            pltpu.VMEM((count * rows, 2 * NF), jnp.bfloat16),
            pltpu.VMEM(block, jnp.float32),
            pltpu.VMEM(block, jnp.float32),
            pltpu.SemaphoreType.DMA((count,)),
            pltpu.SemaphoreType.DMA((count,)),
        ],
        compiler_params=pltpu.CompilerParams(vmem_limit_bytes=12 << 20),
        cost_estimate=pl.CostEstimate(flops=count << 30, bytes_accessed=1 << 22, transcendentals=0),
    )(*args)


def local(panels, routes, stack_in):
    n_z = lax.axis_size("z")
    n_x = lax.axis_size("x")
    payload = whiten(panels[0], routes[0])
    column = lax.all_gather(payload, "z", axis=0, tiled=False)
    column = column.transpose(1, 0, 2, 3).reshape(SLICES + 1, n_z * CH, LANES)
    hops = (0, 1, 3, 2)
    sources = [column]
    for hop in hops[1:]:
        pairs = [(i, (i + hop) % n_x) for i in range(n_x)]
        sources.append(lax.ppermute(column, "x", pairs))
    peers = lax.axis_size(("y", "core"))
    copies = jnp.broadcast_to(payload[None, :SLICES], (peers, SLICES, CH, LANES))
    group = lax.all_to_all(copies, ("y", "core"), split_axis=0, concat_axis=0, tiled=True)
    receivers = group.transpose(0, 2, 1, 3).reshape(-1, LANES).astype(jnp.float32)
    steering = steer(receivers, tables())
    partial = stack(hops[:3], sources[:3], steering, stack_in[0, 0])
    return stack(hops[3:], sources[3:], steering, stack_in[0, 0], partial)[None, None]


def solution(mesh):
    grid = Mesh(mesh.devices.reshape(-1, 2, 4, 16), ("y", "core", "x", "z"))
    grp, blk = ("y", "core"), ("x", "z")
    return jax.shard_map(
        local,
        mesh=grid,
        in_specs=(P(blk, grp, None), P(blk, grp, None), P(grp, blk, None, None, None)),
        out_specs=P(grp, blk, None, None, None),
        check_vma=False,
    )
```

```python
import functools
import math

import jax
import jax.numpy as jnp
import numpy as np
from jax import lax
from jax.experimental import pallas as pl
from jax.experimental.pallas import tpu as pltpu
from jax.sharding import Mesh, PartitionSpec as P

NF = 4096
LAGS = 128
SMOOTH = 64
LANES = 128
SLICES = 2 * NF // LANES
CH = 2
DEPTH = 2048
ROUTE_LANES = 128


def make_table():
    frequency = np.arange(NF, dtype=np.int64)[:, None]
    lag = np.arange(LAGS)[None, :] - LAGS // 2
    angle = (frequency * lag % (2 * NF)) * (math.pi / NF)
    table = np.concatenate([np.cos(angle), -np.sin(angle)])
    return table.astype(np.float32).astype(jnp.bfloat16)


def whiten_kernel(panels_ref, routes_ref, out_ref, copies_ref, rows_ref):
    real = panels_ref[:, :NF]
    imag = panels_ref[:, NF:]
    amplitude = jnp.sqrt(real * real + imag * imag)
    wide = NF + 2 * SMOOTH
    padded = jnp.concatenate([amplitude, jnp.zeros((CH, 2 * SMOOTH), jnp.float32)], axis=1)
    total = padded
    span = 1
    while span < 2 * SMOOTH:
        total = total + pltpu.roll(total, span, 1)
        span *= 2
    total = total + pltpu.roll(padded, 2 * SMOOTH, 1)
    total = pltpu.roll(total, wide - SMOOTH, 1)[:, :NF]
    divisor = total / (2 * SMOOTH + 1) + 1e-06
    half = SLICES // 2
    for base, value in ((0, real / divisor), (half, imag / divisor)):
        for j in range(half):
            piece = value[:, j * LANES : (j + 1) * LANES]
            out_ref[base + j] = piece.astype(jnp.bfloat16)
            for k in range(CH):
                rows_ref[pl.ds(k * SLICES + base + j, 1), :] = piece[k : k + 1]
    routes = routes_ref[...].astype(jnp.float32)
    rest = jnp.full((CH, ROUTE_LANES - routes.shape[1]), -1.0, jnp.float32)
    out_ref[SLICES] = jnp.concatenate([routes, rest], axis=1).astype(jnp.bfloat16)
    own = rows_ref[...].astype(jnp.bfloat16)
    for p in range(copies_ref.shape[0]):
        copies_ref[p] = own


def whiten(panels, routes, peers):
    return pl.pallas_call(
        whiten_kernel,
        out_shape=[
            jax.ShapeDtypeStruct((SLICES + 1, CH, LANES), jnp.bfloat16),
            jax.ShapeDtypeStruct((peers, CH * SLICES, LANES), jnp.bfloat16),
        ],
        scratch_shapes=[pltpu.VMEM((CH * SLICES, LANES), jnp.float32)],
        cost_estimate=pl.CostEstimate(flops=1 << 20, bytes_accessed=400000, transcendentals=0),
    )(panels, routes)


def stack_kernel(hops, first, *refs):
    count = len(hops)
    parts = refs[:count]
    recv_ref, table_in, stack_ref = refs[count : count + 3]
    refs = refs[count + 3 + (not first) :]
    if first:
        out_ref, table_ref, wide_ref, after_ref, out_sem, table_sem = refs
    else:
        out_ref, wide_ref, after_ref, out_sem = refs
        table_ref = table_in
    rows = parts[0].shape[1]
    receivers = recv_ref.shape[0] // SLICES
    half = SLICES // 2
    steps = NF // DEPTH
    per = DEPTH // LANES
    x = lax.axis_index("x")
    n_x = lax.axis_size("x")
    owner = x * lax.axis_size("z") + lax.axis_index("z")
    places = [pl.ds(lax.rem(x + n_x - hop, n_x) * rows, rows) for hop in hops]

    def fetch(q, h):
        piece = pl.ds(h * NF + q * DEPTH, DEPTH)
        return pltpu.make_async_copy(table_in.at[piece], table_ref.at[piece], table_sem.at[2 * q + h])

    def write(i):
        return pltpu.make_async_copy(after_ref.at[i], out_ref.at[places[i]], out_sem.at[i])

    if first:
        for q in range(steps):
            for h in range(2):
                fetch(q, h).start()

    for i, part in enumerate(parts):
        for j in range(SLICES):
            wide_ref[j] = part[j].astype(jnp.float32)
        sums = jnp.zeros((rows * receivers, LAGS), jnp.float32)
        for q in range(steps):
            real, imag = [], []
            for u in range(per):
                j = q * per + u
                rr = recv_ref[pl.ds(j, receivers, stride=SLICES), :]
                ri = recv_ref[pl.ds(half + j, receivers, stride=SLICES), :]
                re, im = [], []
                for s in range(rows):
                    sr = jnp.broadcast_to(wide_ref[j, pl.ds(s, 1), :], rr.shape)
                    si = jnp.broadcast_to(wide_ref[half + j, pl.ds(s, 1), :], rr.shape)
                    re.append((sr * rr + si * ri).astype(jnp.bfloat16))
                    im.append((si * rr - sr * ri).astype(jnp.bfloat16))
                real.append(jnp.concatenate(re, axis=0))
                imag.append(jnp.concatenate(im, axis=0))
            for h, value in enumerate((real, imag)):
                if first and i == 0:
                    fetch(q, h).wait()
                weights = table_ref[h * NF + q * DEPTH : h * NF + (q + 1) * DEPTH, :]
                sums = sums + jnp.dot(
                    jnp.concatenate(value, axis=1), weights, preferred_element_type=jnp.float32
                )
        routes = part[SLICES].astype(jnp.float32)
        named = jnp.where(routes == owner.astype(jnp.float32), 1.0, 0.0)
        scale = jnp.max(named, axis=1, keepdims=True) * (1.0 / math.sqrt(NF))
        block = sums.reshape(rows, receivers, LAGS) * scale[:, :, None]
        after_ref[i] = stack_ref[places[i]] + block
        write(i).start()
    for i in range(count):
        write(i).wait()


def stack(hops, sources, receivers, table, previous, partial=None):
    first = partial is None
    count = len(hops)
    rows = sources[0].shape[1]
    vmem, other = pl.BlockSpec(memory_space=pltpu.VMEM), pl.BlockSpec(memory_space=pl.ANY)
    args = [*sources, receivers, table, previous] + ([] if first else [partial])
    shapes = [jax.ShapeDtypeStruct(previous.shape, jnp.float32)]
    semaphores = [pltpu.SemaphoreType.DMA((count,))]
    if first:
        shapes.append(pltpu.VMEM(table.shape, table.dtype))
        semaphores.append(pltpu.SemaphoreType.DMA((2 * NF // DEPTH,)))
        args[count + 1] = pltpu.with_memory_space_constraint(table, pltpu.HBM)
    return pl.pallas_call(
        functools.partial(stack_kernel, hops, first),
        out_shape=shapes,
        in_specs=[vmem] * (count + 1)
        + [pl.BlockSpec(memory_space=pltpu.HBM) if first else vmem, vmem]
        + ([] if first else [other]),
        out_specs=[other] + ([vmem] if first else []),
        input_output_aliases={} if first else {len(args) - 1: 0},
        scratch_shapes=[
            pltpu.VMEM((SLICES, rows, LANES), jnp.float32),
            pltpu.VMEM((count, rows) + previous.shape[1:], jnp.float32),
            *semaphores,
        ],
        compiler_params=pltpu.CompilerParams(vmem_limit_bytes=40 << 20),
        cost_estimate=pl.CostEstimate(flops=count << 30, bytes_accessed=1 << 22, transcendentals=0),
    )(*args)


def local(panels, routes, stack_in):
    n_z = lax.axis_size("z")
    n_x = lax.axis_size("x")
    group = ("y", "core")
    payload, copies = whiten(panels[0], routes[0], lax.axis_size(group))
    column = lax.all_gather(payload, "z", axis=0, tiled=False)
    column = column.transpose(1, 0, 2, 3).reshape(SLICES + 1, n_z * CH, LANES)
    hops = (0, 1, 3, 2)
    sources = [column]
    for hop in hops[1:]:
        pairs = [(i, (i + hop) % n_x) for i in range(n_x)]
        sources.append(lax.ppermute(column, "x", pairs))
    receivers = lax.all_to_all(copies, group, split_axis=0, concat_axis=0, tiled=True)
    receivers = receivers.reshape(-1, LANES).astype(jnp.float32)
    previous = stack_in[0, 0]
    partial, table = stack(hops[:3], sources[:3], receivers, make_table(), previous)
    (stacked,) = stack(hops[3:], sources[3:], receivers, table, previous, partial)
    return stacked[None, None]


def solution(mesh):
    grid = Mesh(mesh.devices.reshape(-1, 2, 4, 16), ("y", "core", "x", "z"))
    grp, blk = ("y", "core"), ("x", "z")
    return jax.shard_map(
        local,
        mesh=grid,
        in_specs=(P(blk, grp, None), P(blk, grp, None), P(grp, blk, None, None, None)),
        out_specs=P(grp, blk, None, None, None),
        check_vma=False,
    )
```

```python
import functools
import math

import jax
import jax.numpy as jnp
import numpy as np
from jax import lax
from jax.experimental import pallas as pl
from jax.experimental.pallas import tpu as pltpu
from jax.sharding import Mesh, PartitionSpec as P

NF = 4096
LAGS = 128
SMOOTH = 64
LANES = 128
SLICES = 2 * NF // LANES
CH = 2
DEPTH = 4096
ROUTE_LANES = 128


def make_table():
    frequency = np.arange(NF, dtype=np.int64)[:, None]
    lag = np.arange(LAGS)[None, :] - LAGS // 2
    angle = (frequency * lag % (2 * NF)) * (math.pi / NF)
    table = np.concatenate([np.cos(angle), -np.sin(angle)])
    return table.astype(np.float32).astype(jnp.bfloat16)


def whiten_kernel(panels_ref, routes_ref, out_ref, copies_ref, rows_ref):
    real = panels_ref[:, :NF]
    imag = panels_ref[:, NF:]
    amplitude = jnp.sqrt(real * real + imag * imag)
    wide = NF + 2 * SMOOTH
    padded = jnp.concatenate([amplitude, jnp.zeros((CH, 2 * SMOOTH), jnp.float32)], axis=1)
    total = padded
    span = 1
    while span < 2 * SMOOTH:
        total = total + pltpu.roll(total, span, 1)
        span *= 2
    total = total + pltpu.roll(padded, 2 * SMOOTH, 1)
    total = pltpu.roll(total, wide - SMOOTH, 1)[:, :NF]
    divisor = total / (2 * SMOOTH + 1) + 1e-06
    half = SLICES // 2
    for base, value in ((0, real / divisor), (half, imag / divisor)):
        for j in range(half):
            piece = value[:, j * LANES : (j + 1) * LANES]
            out_ref[base + j] = piece.astype(jnp.bfloat16)
            for k in range(CH):
                rows_ref[pl.ds(k * SLICES + base + j, 1), :] = piece[k : k + 1]
    routes = routes_ref[...].astype(jnp.float32)
    rest = jnp.full((CH, ROUTE_LANES - routes.shape[1]), -1.0, jnp.float32)
    out_ref[SLICES] = jnp.concatenate([routes, rest], axis=1).astype(jnp.bfloat16)
    own = rows_ref[...].astype(jnp.bfloat16)
    for p in range(copies_ref.shape[0]):
        copies_ref[p] = own


def whiten(panels, routes, peers):
    return pl.pallas_call(
        whiten_kernel,
        out_shape=[
            pltpu.VMEM((SLICES + 1, CH, LANES), jnp.bfloat16),
            pltpu.VMEM((peers, CH * SLICES, LANES), jnp.bfloat16),
        ],
        in_specs=[pl.BlockSpec(memory_space=pltpu.VMEM)] * 2,
        out_specs=[pl.BlockSpec(memory_space=pltpu.VMEM)] * 2,
        scratch_shapes=[pltpu.VMEM((CH * SLICES, LANES), jnp.float32)],
        cost_estimate=pl.CostEstimate(flops=1 << 20, bytes_accessed=400000, transcendentals=0),
    )(panels, routes)


def stack_kernel(hops, load, earlier, *refs):
    count = len(hops)
    held = len(earlier)
    parts = refs[:count]
    recv_ref, table_in, stack_ref = refs[count : count + 3]
    earlier_refs = refs[count + 3 : count + 3 + held]
    refs = list(refs[count + 3 + held :])
    out_ref = refs.pop(0)
    table_ref = refs.pop(0) if load else table_in
    wide_ref = refs.pop(0)
    if held:
        after_ref, out_sem = refs
    else:
        after_ref = out_ref
    table_sem = refs[-1] if load else None
    rows = parts[0].shape[1]
    receivers = recv_ref.shape[0] // SLICES
    half = SLICES // 2
    steps = NF // DEPTH
    per = DEPTH // LANES
    x = lax.axis_index("x")
    n_x = lax.axis_size("x")
    owner = x * lax.axis_size("z") + lax.axis_index("z")

    def place(hop):
        return pl.ds(lax.rem(x + n_x - hop, n_x) * rows, rows)

    def fetch(q, h):
        piece = pl.ds(h * NF + q * DEPTH, DEPTH)
        return pltpu.make_async_copy(table_in.at[piece], table_ref.at[piece], table_sem.at[2 * q + h])

    writes = []
    if load:
        for q in range(steps):
            for h in range(2):
                fetch(q, h).start()
    for ref, their_hops in zip(earlier_refs, earlier):
        for i, hop in enumerate(their_hops):
            writes.append(pltpu.make_async_copy(ref.at[i], out_ref.at[place(hop)], out_sem.at[len(writes)]))
            writes[-1].start()

    for i, part in enumerate(parts):
        routes = part[SLICES].astype(jnp.float32)
        named = jnp.where(routes == owner.astype(jnp.float32), 1.0, 0.0)
        live = jnp.broadcast_to(jnp.max(named, axis=1, keepdims=True), routes.shape)
        for j in range(SLICES):
            wide_ref[j] = part[j].astype(jnp.float32) * live
        sums = jnp.zeros((rows * receivers, LAGS), jnp.float32)
        for q in range(steps):
            real, imag = [], []
            for u in range(per):
                j = q * per + u
                rr = recv_ref[pl.ds(j, receivers, stride=SLICES), :]
                ri = recv_ref[pl.ds(half + j, receivers, stride=SLICES), :]
                re, im = [], []
                for s in range(rows):
                    sr = jnp.broadcast_to(wide_ref[j, pl.ds(s, 1), :], rr.shape)
                    si = jnp.broadcast_to(wide_ref[half + j, pl.ds(s, 1), :], rr.shape)
                    re.append((sr * rr + si * ri).astype(jnp.bfloat16))
                    im.append((si * rr - sr * ri).astype(jnp.bfloat16))
                real.append(jnp.concatenate(re, axis=0))
                imag.append(jnp.concatenate(im, axis=0))
            for h, value in enumerate((real, imag)):
                if load and i == 0:
                    fetch(q, h).wait()
                weights = table_ref[h * NF + q * DEPTH : h * NF + (q + 1) * DEPTH, :]
                sums = sums + jnp.dot(
                    jnp.concatenate(value, axis=1), weights, preferred_element_type=jnp.float32
                )
        block = sums.reshape(rows, receivers, LAGS) * (1.0 / math.sqrt(NF))
        after_ref[i] = stack_ref[place(hops[i])] + block
        if held:
            writes.append(
                pltpu.make_async_copy(after_ref.at[i], out_ref.at[place(hops[i])], out_sem.at[len(writes)])
            )
            writes[-1].start()
    for copy in writes:
        copy.wait()


def stack(hops, sources, receivers, table, previous, load=False, earlier=()):
    count = len(hops)
    rows = sources[0].shape[1]
    vmem = pl.BlockSpec(memory_space=pltpu.VMEM)
    block = (count, rows) + previous.shape[1:]
    if load:
        table = pltpu.with_memory_space_constraint(table, pltpu.HBM)
    scratch = [pltpu.VMEM((SLICES, rows, LANES), jnp.float32)]
    if earlier:
        shapes = [jax.ShapeDtypeStruct(previous.shape, jnp.float32)]
        total = count + sum(len(h) for h, _ in earlier)
        scratch += [pltpu.VMEM(block, jnp.float32), pltpu.SemaphoreType.DMA((total,))]
    else:
        shapes = [pltpu.VMEM(block, jnp.float32)]
    if load:
        shapes.append(pltpu.VMEM(table.shape, jnp.bfloat16))
        scratch.append(pltpu.SemaphoreType.DMA((2 * NF // DEPTH,)))
    return pl.pallas_call(
        functools.partial(stack_kernel, hops, load, tuple(h for h, _ in earlier)),
        out_shape=shapes,
        in_specs=[vmem] * (count + 1)
        + [pl.BlockSpec(memory_space=pltpu.HBM) if load else vmem, vmem]
        + [vmem] * len(earlier),
        out_specs=[pl.BlockSpec(memory_space=pl.ANY) if earlier else vmem] + ([vmem] if load else []),
        scratch_shapes=scratch,
        compiler_params=pltpu.CompilerParams(vmem_limit_bytes=40 << 20),
        cost_estimate=pl.CostEstimate(flops=count << 30, bytes_accessed=1 << 22, transcendentals=0),
    )(*sources, receivers, table, previous, *(r for _, r in earlier))


def local(panels, routes, stack_in):
    n_z = lax.axis_size("z")
    n_x = lax.axis_size("x")
    group = ("y", "core")
    payload, copies = whiten(panels[0], routes[0], lax.axis_size(group))
    column = lax.all_gather(payload, "z", axis=0, tiled=False)
    column = column.transpose(1, 0, 2, 3).reshape(SLICES + 1, n_z * CH, LANES)
    hops = (0, 1, 3, 2)
    sources = [column]
    for hop in hops[1:]:
        pairs = [(i, (i + hop) % n_x) for i in range(n_x)]
        sources.append(lax.ppermute(column, "x", pairs))
    receivers = lax.all_to_all(copies, group, split_axis=0, concat_axis=0, tiled=True)
    receivers = receivers.reshape(-1, LANES).astype(jnp.float32)
    previous = stack_in[0, 0]
    early, table = stack(hops[:2], sources[:2], receivers, make_table(), previous, load=True)
    (middle,) = stack(hops[2:3], sources[2:3], receivers, table, previous)
    earlier = ((hops[:2], early), (hops[2:3], middle))
    (stacked,) = stack(hops[3:], sources[3:], receivers, table, previous, earlier=earlier)
    return stacked[None, None]


def solution(mesh):
    grid = Mesh(mesh.devices.reshape(-1, 2, 4, 16), ("y", "core", "x", "z"))
    grp, blk = ("y", "core"), ("x", "z")
    return jax.shard_map(
        local,
        mesh=grid,
        in_specs=(P(blk, grp, None), P(blk, grp, None), P(grp, blk, None, None, None)),
        out_specs=P(grp, blk, None, None, None),
        check_vma=False,
    )
```

```python
import functools
import math

import jax
import jax.numpy as jnp
import numpy as np
from jax import lax
from jax.experimental import pallas as pl
from jax.experimental.pallas import tpu as pltpu
from jax.sharding import Mesh, PartitionSpec as P

NF = 4096
LAGS = 128
SMOOTH = 64
LANES = 128
SLICES = 2 * NF // LANES
CH = 2
DEPTH = 4096
ROUTE_LANES = 128


def make_table():
    frequency = np.arange(NF, dtype=np.int64)[:, None]
    lag = np.arange(LAGS)[None, :] - LAGS // 2
    angle = (frequency * lag % (2 * NF)) * (math.pi / NF)
    table = np.concatenate([np.cos(angle), -np.sin(angle)])
    return table.astype(np.float32).astype(jnp.bfloat16)


def whiten_kernel(panels_ref, routes_ref, out_ref, copies_ref, rows_ref):
    real = panels_ref[:, :NF]
    imag = panels_ref[:, NF:]
    amplitude = jnp.sqrt(real * real + imag * imag)
    wide = NF + 2 * SMOOTH
    padded = jnp.concatenate([amplitude, jnp.zeros((CH, 2 * SMOOTH), jnp.float32)], axis=1)
    total = padded
    span = 1
    while span < 2 * SMOOTH:
        total = total + pltpu.roll(total, span, 1)
        span *= 2
    total = total + pltpu.roll(padded, 2 * SMOOTH, 1)
    total = pltpu.roll(total, wide - SMOOTH, 1)[:, :NF]
    divisor = total / (2 * SMOOTH + 1) + 1e-06
    half = SLICES // 2
    for base, value in ((0, real / divisor), (half, imag / divisor)):
        for j in range(half):
            piece = value[:, j * LANES : (j + 1) * LANES]
            out_ref[base + j] = piece.astype(jnp.bfloat16)
            for k in range(CH):
                rows_ref[pl.ds(k * SLICES + base + j, 1), :] = piece[k : k + 1]
    routes = routes_ref[...].astype(jnp.float32)
    rest = jnp.full((CH, ROUTE_LANES - routes.shape[1]), -1.0, jnp.float32)
    out_ref[SLICES] = jnp.concatenate([routes, rest], axis=1).astype(jnp.bfloat16)
    own = rows_ref[...].astype(jnp.bfloat16)
    for p in range(copies_ref.shape[0]):
        copies_ref[p] = own


def whiten(panels, routes, peers):
    return pl.pallas_call(
        whiten_kernel,
        out_shape=[
            pltpu.VMEM((SLICES + 1, CH, LANES), jnp.bfloat16),
            pltpu.VMEM((peers, CH * SLICES, LANES), jnp.bfloat16),
        ],
        in_specs=[pl.BlockSpec(memory_space=pltpu.VMEM)] * 2,
        out_specs=[pl.BlockSpec(memory_space=pltpu.VMEM)] * 2,
        scratch_shapes=[pltpu.VMEM((CH * SLICES, LANES), jnp.float32)],
        cost_estimate=pl.CostEstimate(flops=1 << 20, bytes_accessed=400000, transcendentals=0),
    )(panels, routes)


def stack_kernel(hops, load, earlier, *refs):
    count = len(hops)
    held = len(earlier)
    parts = refs[:count]
    recv_ref, table_in, stack_ref = refs[count : count + 3]
    earlier_refs = refs[count + 3 : count + 3 + held]
    refs = list(refs[count + 3 + held :])
    out_ref = refs.pop(0)
    table_ref = refs.pop(0) if load else table_in
    wide_ref = refs.pop(0)
    if held:
        after_ref, out_sem = refs
    else:
        after_ref = out_ref
    table_sem = refs[-1] if load else None
    rows = parts[0].shape[1]
    receivers = recv_ref.shape[0] // SLICES
    half = SLICES // 2
    steps = NF // DEPTH
    per = DEPTH // LANES
    x = lax.axis_index("x")
    n_x = lax.axis_size("x")
    owner = x * lax.axis_size("z") + lax.axis_index("z")

    def place(hop):
        return pl.ds(lax.rem(x + n_x - hop, n_x) * rows, rows)

    def fetch(q, h):
        piece = pl.ds(h * NF + q * DEPTH, DEPTH)
        return pltpu.make_async_copy(table_in.at[piece], table_ref.at[piece], table_sem.at[2 * q + h])

    writes = []
    if load:
        for q in range(steps):
            for h in range(2):
                fetch(q, h).start()
    for ref, their_hops in zip(earlier_refs, earlier):
        for i, hop in enumerate(their_hops):
            writes.append(pltpu.make_async_copy(ref.at[i], out_ref.at[place(hop)], out_sem.at[len(writes)]))
            writes[-1].start()

    for i, part in enumerate(parts):
        routes = part[SLICES].astype(jnp.float32)
        named = jnp.where(routes == owner.astype(jnp.float32), 1.0, 0.0)
        live = jnp.broadcast_to(jnp.max(named, axis=1, keepdims=True), routes.shape)
        for j in range(SLICES):
            wide_ref[j] = part[j].astype(jnp.float32) * live
        sums = jnp.zeros((rows * receivers, LAGS), jnp.float32)
        for q in range(steps):
            real, imag = [], []
            for u in range(per):
                j = q * per + u
                rr = recv_ref[pl.ds(j, receivers, stride=SLICES), :]
                ri = recv_ref[pl.ds(half + j, receivers, stride=SLICES), :]
                re, im = [], []
                for s in range(rows):
                    sr = jnp.broadcast_to(wide_ref[j, pl.ds(s, 1), :], rr.shape)
                    si = jnp.broadcast_to(wide_ref[half + j, pl.ds(s, 1), :], rr.shape)
                    re.append((sr * rr + si * ri).astype(jnp.bfloat16))
                    im.append((si * rr - sr * ri).astype(jnp.bfloat16))
                real.append(jnp.concatenate(re, axis=0))
                imag.append(jnp.concatenate(im, axis=0))
            for h, value in enumerate((real, imag)):
                if load and i == 0:
                    fetch(q, h).wait()
                weights = table_ref[h * NF + q * DEPTH : h * NF + (q + 1) * DEPTH, :]
                sums = sums + jnp.dot(
                    jnp.concatenate(value, axis=1), weights, preferred_element_type=jnp.float32
                )
        block = sums.reshape(rows, receivers, LAGS) * (1.0 / math.sqrt(NF))
        after_ref[i] = stack_ref[place(hops[i])] + block
        if held:
            writes.append(
                pltpu.make_async_copy(after_ref.at[i], out_ref.at[place(hops[i])], out_sem.at[len(writes)])
            )
            writes[-1].start()
    for copy in writes:
        copy.wait()


def stack(hops, sources, receivers, table, previous, load=False, earlier=()):
    count = len(hops)
    rows = sources[0].shape[1]
    vmem = pl.BlockSpec(memory_space=pltpu.VMEM)
    block = (count, rows) + previous.shape[1:]
    if load:
        table = pltpu.with_memory_space_constraint(table, pltpu.HBM)
    scratch = [pltpu.VMEM((SLICES, rows, LANES), jnp.float32)]
    if earlier:
        shapes = [jax.ShapeDtypeStruct(previous.shape, jnp.float32)]
        total = count + sum(len(h) for h, _ in earlier)
        scratch += [pltpu.VMEM(block, jnp.float32), pltpu.SemaphoreType.DMA((total,))]
    else:
        shapes = [pltpu.VMEM(block, jnp.float32)]
    if load:
        shapes.append(pltpu.VMEM(table.shape, jnp.bfloat16))
        scratch.append(pltpu.SemaphoreType.DMA((2 * NF // DEPTH,)))
    return pl.pallas_call(
        functools.partial(stack_kernel, hops, load, tuple(h for h, _ in earlier)),
        out_shape=shapes,
        in_specs=[vmem] * (count + 1)
        + [pl.BlockSpec(memory_space=pltpu.HBM) if load else vmem, vmem]
        + [vmem] * len(earlier),
        out_specs=[pl.BlockSpec(memory_space=pl.ANY) if earlier else vmem] + ([vmem] if load else []),
        scratch_shapes=scratch,
        compiler_params=pltpu.CompilerParams(vmem_limit_bytes=40 << 20),
        cost_estimate=pl.CostEstimate(flops=count << 30, bytes_accessed=1 << 22, transcendentals=0),
    )(*sources, receivers, table, previous, *(r for _, r in earlier))


def local(panels, routes, stack_in):
    n_z = lax.axis_size("z")
    n_x = lax.axis_size("x")
    group = ("y", "core")
    payload, copies = whiten(panels[0], routes[0], lax.axis_size(group))
    column = lax.all_gather(payload, "z", axis=0, tiled=False)
    column = column.transpose(1, 0, 2, 3).reshape(SLICES + 1, n_z * CH, LANES)
    hops = (0, 2, 1, 3)
    sources = [column]
    for hop in hops[1:]:
        pairs = [(i, (i + hop) % n_x) for i in range(n_x)]
        sources.append(lax.ppermute(column, "x", pairs))
    receivers = lax.all_to_all(copies, group, split_axis=0, concat_axis=0, tiled=True)
    receivers = receivers.reshape(-1, LANES).astype(jnp.float32)
    previous = stack_in[0, 0]
    early, table = stack(hops[:2], sources[:2], receivers, make_table(), previous, load=True)
    (middle,) = stack(hops[2:3], sources[2:3], receivers, table, previous)
    earlier = ((hops[:2], early), (hops[2:3], middle))
    (stacked,) = stack(hops[3:], sources[3:], receivers, table, previous, earlier=earlier)
    return stacked[None, None]


def solution(mesh):
    grid = Mesh(mesh.devices.reshape(-1, 2, 4, 16), ("y", "core", "x", "z"))
    grp, blk = ("y", "core"), ("x", "z")
    return jax.shard_map(
        local,
        mesh=grid,
        in_specs=(P(blk, grp, None), P(blk, grp, None), P(grp, blk, None, None, None)),
        out_specs=P(grp, blk, None, None, None),
        check_vma=False,
    )
```

```python
import functools
import math

import jax
import jax.numpy as jnp
import numpy as np
from jax import lax
from jax.experimental import pallas as pl
from jax.experimental.pallas import tpu as pltpu
from jax.sharding import Mesh, PartitionSpec as P

NF = 4096
LAGS = 128
SMOOTH = 64
LANES = 128
SLICES = 2 * NF // LANES
CH = 2
DEPTH = 4096
ROUTE_LANES = 128


def make_table():
    frequency = np.arange(NF, dtype=np.int64)[:, None]
    lag = np.arange(LAGS)[None, :] - LAGS // 2
    angle = (frequency * lag % (2 * NF)) * (math.pi / NF)
    table = np.concatenate([np.cos(angle), -np.sin(angle)])
    return table.astype(np.float32).astype(jnp.bfloat16)


def whiten_kernel(panels_ref, routes_ref, out_ref, copies_ref, rows_ref):
    real = panels_ref[:, :NF]
    imag = panels_ref[:, NF:]
    amplitude = jnp.sqrt(real * real + imag * imag)
    wide = NF + 2 * SMOOTH
    padded = jnp.concatenate([amplitude, jnp.zeros((CH, 2 * SMOOTH), jnp.float32)], axis=1)
    total = padded
    span = 1
    while span < 2 * SMOOTH:
        total = total + pltpu.roll(total, span, 1)
        span *= 2
    total = total + pltpu.roll(padded, 2 * SMOOTH, 1)
    total = pltpu.roll(total, wide - SMOOTH, 1)[:, :NF]
    divisor = total / (2 * SMOOTH + 1) + 1e-06
    half = SLICES // 2
    for base, value in ((0, real / divisor), (half, imag / divisor)):
        for j in range(half):
            piece = value[:, j * LANES : (j + 1) * LANES]
            out_ref[base + j] = piece.astype(jnp.bfloat16)
            for k in range(CH):
                rows_ref[pl.ds(k * SLICES + base + j, 1), :] = piece[k : k + 1]
    routes = routes_ref[...].astype(jnp.float32)
    rest = jnp.full((CH, ROUTE_LANES - routes.shape[1]), -1.0, jnp.float32)
    out_ref[SLICES] = jnp.concatenate([routes, rest], axis=1).astype(jnp.bfloat16)
    own = rows_ref[...].astype(jnp.bfloat16)
    for p in range(copies_ref.shape[0]):
        copies_ref[p] = own


def whiten(panels, routes, peers):
    return pl.pallas_call(
        whiten_kernel,
        out_shape=[
            pltpu.VMEM((SLICES + 1, CH, LANES), jnp.bfloat16),
            pltpu.VMEM((peers, CH * SLICES, LANES), jnp.bfloat16),
        ],
        in_specs=[pl.BlockSpec(memory_space=pltpu.VMEM)] * 2,
        out_specs=[pl.BlockSpec(memory_space=pltpu.VMEM)] * 2,
        scratch_shapes=[pltpu.VMEM((CH * SLICES, LANES), jnp.float32)],
        cost_estimate=pl.CostEstimate(flops=1 << 20, bytes_accessed=400000, transcendentals=0),
    )(panels, routes)


def stack_kernel(hops, load, earlier, *refs):
    count = len(hops)
    held = len(earlier)
    parts = refs[:count]
    recv_ref, table_in, stack_ref = refs[count : count + 3]
    earlier_refs = refs[count + 3 : count + 3 + held]
    refs = list(refs[count + 3 + held :])
    out_ref = refs.pop(0)
    table_ref = refs.pop(0) if load else table_in
    wide_ref = refs.pop(0)
    if held:
        after_ref, out_sem = refs
    else:
        after_ref = out_ref
    table_sem = refs[-1] if load else None
    rows = parts[0].shape[1]
    receivers = recv_ref.shape[0] // SLICES
    half = SLICES // 2
    steps = NF // DEPTH
    per = DEPTH // LANES
    x = lax.axis_index("x")
    n_x = lax.axis_size("x")
    owner = x * lax.axis_size("z") + lax.axis_index("z")

    def place(hop):
        return pl.ds(lax.rem(x + n_x - hop, n_x) * rows, rows)

    def fetch(q, h):
        piece = pl.ds(h * NF + q * DEPTH, DEPTH)
        return pltpu.make_async_copy(table_in.at[piece], table_ref.at[piece], table_sem.at[2 * q + h])

    writes = []
    if load:
        for q in range(steps):
            for h in range(2):
                fetch(q, h).start()
    for ref, their_hops in zip(earlier_refs, earlier):
        for i, hop in enumerate(their_hops):
            writes.append(pltpu.make_async_copy(ref.at[i], out_ref.at[place(hop)], out_sem.at[len(writes)]))
            writes[-1].start()

    for i, part in enumerate(parts):
        routes = part[SLICES].astype(jnp.float32)
        named = jnp.where(routes == owner.astype(jnp.float32), 1.0, 0.0)
        live = jnp.broadcast_to(jnp.max(named, axis=1, keepdims=True), routes.shape)
        for j in range(SLICES):
            wide_ref[j] = part[j].astype(jnp.float32) * live
        if load and i == 0:
            for q in range(steps):
                for h in range(2):
                    fetch(q, h).wait()
        sums = jnp.zeros((rows * receivers, LAGS), jnp.float32)
        for q in range(steps):
            real, imag = [], []
            for u in range(per):
                j = q * per + u
                rr = recv_ref[pl.ds(j, receivers, stride=SLICES), :]
                ri = recv_ref[pl.ds(half + j, receivers, stride=SLICES), :]
                re, im = [], []
                for s in range(rows):
                    sr = jnp.broadcast_to(wide_ref[j, pl.ds(s, 1), :], rr.shape)
                    si = jnp.broadcast_to(wide_ref[half + j, pl.ds(s, 1), :], rr.shape)
                    re.append((sr * rr + si * ri).astype(jnp.bfloat16))
                    im.append((si * rr - sr * ri).astype(jnp.bfloat16))
                real.append(jnp.concatenate(re, axis=0))
                imag.append(jnp.concatenate(im, axis=0))
            for h, value in enumerate((real, imag)):
                weights = table_ref[h * NF + q * DEPTH : h * NF + (q + 1) * DEPTH, :]
                sums = sums + jnp.dot(
                    jnp.concatenate(value, axis=1), weights, preferred_element_type=jnp.float32
                )
        block = sums.reshape(rows, receivers, LAGS) * (1.0 / math.sqrt(NF))
        after_ref[i] = stack_ref[place(hops[i])] + block
        if held:
            writes.append(
                pltpu.make_async_copy(after_ref.at[i], out_ref.at[place(hops[i])], out_sem.at[len(writes)])
            )
            writes[-1].start()
    for copy in writes:
        copy.wait()


def stack(hops, sources, receivers, table, previous, load=False, earlier=()):
    count = len(hops)
    rows = sources[0].shape[1]
    vmem = pl.BlockSpec(memory_space=pltpu.VMEM)
    block = (count, rows) + previous.shape[1:]
    if load:
        table = pltpu.with_memory_space_constraint(table, pltpu.HBM)
    scratch = [pltpu.VMEM((SLICES, rows, LANES), jnp.float32)]
    if earlier:
        shapes = [jax.ShapeDtypeStruct(previous.shape, jnp.float32)]
        total = count + sum(len(h) for h, _ in earlier)
        scratch += [pltpu.VMEM(block, jnp.float32), pltpu.SemaphoreType.DMA((total,))]
    else:
        shapes = [pltpu.VMEM(block, jnp.float32)]
    if load:
        shapes.append(pltpu.VMEM(table.shape, jnp.bfloat16))
        scratch.append(pltpu.SemaphoreType.DMA((2 * NF // DEPTH,)))
    return pl.pallas_call(
        functools.partial(stack_kernel, hops, load, tuple(h for h, _ in earlier)),
        out_shape=shapes,
        in_specs=[vmem] * (count + 1)
        + [pl.BlockSpec(memory_space=pltpu.HBM) if load else vmem, vmem]
        + [vmem] * len(earlier),
        out_specs=[pl.BlockSpec(memory_space=pl.ANY) if earlier else vmem] + ([vmem] if load else []),
        scratch_shapes=scratch,
        compiler_params=pltpu.CompilerParams(vmem_limit_bytes=40 << 20),
        cost_estimate=pl.CostEstimate(flops=count << 30, bytes_accessed=1 << 22, transcendentals=0),
    )(*sources, receivers, table, previous, *(r for _, r in earlier))


def local(panels, routes, stack_in):
    n_z = lax.axis_size("z")
    n_x = lax.axis_size("x")
    group = ("y", "core")
    payload, copies = whiten(panels[0], routes[0], lax.axis_size(group))
    column = lax.all_gather(payload, "z", axis=0, tiled=False)
    column = column.transpose(1, 0, 2, 3).reshape(SLICES + 1, n_z * CH, LANES)
    hops = (0, 1, 3, 2)
    sources = [column]
    for hop in hops[1:]:
        pairs = [(i, (i + hop) % n_x) for i in range(n_x)]
        sources.append(lax.ppermute(column, "x", pairs))
    receivers = lax.all_to_all(copies, group, split_axis=0, concat_axis=0, tiled=True)
    receivers = receivers.reshape(-1, LANES).astype(jnp.float32)
    previous = stack_in[0, 0]
    early, table = stack(hops[:3], sources[:3], receivers, make_table(), previous, load=True)
    earlier = ((hops[:3], early),)
    (stacked,) = stack(hops[3:], sources[3:], receivers, table, previous, earlier=earlier)
    return stacked[None, None]


def solution(mesh):
    grid = Mesh(mesh.devices.reshape(-1, 2, 4, 16), ("y", "core", "x", "z"))
    grp, blk = ("y", "core"), ("x", "z")
    return jax.shard_map(
        local,
        mesh=grid,
        in_specs=(P(blk, grp, None), P(blk, grp, None), P(grp, blk, None, None, None)),
        out_specs=P(grp, blk, None, None, None),
        check_vma=False,
    )
```
